1024 devices in a mesh: grp: 16 (over y, x), bal: 64 (over z, core).
Axes of the slice: x: 4, y: 4, z: 32, core: 2. Of those that a mesh axis runs over, the one named last changes fastest.
Arguments:
- tracers: float32 [2, 64, 64, 16384], P(None, None, 'grp', 'bal'), may hold values from -6 to 6
- winds: bfloat16 [2, 64, 64, 16384], P(None, None, 'grp', 'bal'), may hold values from -16 to 16
- node_mass: float32 [64, 16384], P('grp', 'bal'), may hold values from 0.07 to 5.6
- column_cost: int32 [32, 8192], P('grp', 'bal'), may hold values from 1 to 3, as said below
- weight_in: bfloat16 [256, 1024], replicated, may hold values from -0.375 to 0.375
- weight_out: bfloat16 [1024, 256], replicated, may hold values from -0.1875 to 0.1875
Outputs:
- tracers_next: float32 [2, 64, 64, 16384], P(None, None, 'grp', 'bal')
- columns_out: bfloat16 [4, 64, 32, 8192], P(None, None, 'grp', 'bal')
The draws below stay inside these ranges and needn't reach their ends.
Inputs may be any that keep to these rules, and one draw needn't show every extreme that they name: `column_cost`: among the columns of one index of grp (rows 2 * g to 2 * g + 1 of all columns), exactly a quarter have cost 3 and exactly a quarter cost 2.
All inputs are finite; a program needn't handle non-finite values.
Results may differ from the reference program's by a relative error of at most 0.008.
Values may be sent and summed in bfloat16 or wider, within the bound.
No kernel may reach another device: no remote copies, remote signals or barrier semaphores. Data moves between devices by JAX's collectives and lax.ppermute only.
A program may use at most 32 MiB of HBM per device.

```python
import math
import jax
import jax.numpy as jnp
from jax import lax

EX = 1
EY = 64
LEV = 64
HID = 1024
NEX = 16
NEY = 4096
COLS = 256
N_GRP = 16
N_BAL = 64


def draw_column_cost(key, part):
    per_device = 4 * EX * EY
    members = per_device * N_BAL
    key_bias = jax.random.fold_in(key, 11)
    key_fine = jax.random.fold_in(key, 23)
    device_bias = jax.random.randint(key_bias, (N_GRP, N_BAL, 1), 0, 4)
    fine_bits = jax.random.randint(key_fine, (N_GRP, N_BAL, per_device), 0, 2048)
    position = jnp.arange(members, dtype=jnp.int32).reshape(1, N_BAL, per_device)
    scores = (device_bias * 2048 + fine_bits) * members + position
    flat_scores = scores.reshape(N_GRP, members)
    sorted_order = jnp.argsort(-flat_scores, axis=1)
    ranking = jnp.argsort(sorted_order, axis=1)
    costs_flat = jnp.where(ranking < members // 4, 3, jnp.where(ranking < members // 2, 2, 1)).astype(jnp.int32)
    blocks = costs_flat.reshape(N_GRP, N_BAL, 2 * EX, 2 * EY)
    return blocks.transpose(0, 2, 1, 3).reshape(N_GRP * 2 * EX, N_BAL * 2 * EY)


def draw_winds(key, part):
    layout = (2, LEV, 4 * NEX, 4 * NEY)
    key_sign = jax.random.fold_in(key, 101)
    key_size = jax.random.fold_in(key, 103)
    signs = jax.random.randint(key_sign, layout, 0, 2).astype(jnp.float32) * 2.0 - 1.0
    magnitude = jax.random.uniform(key_size, layout, jnp.float32, 10.0, 16.0)
    return (signs * magnitude).astype(jnp.bfloat16)


def draw_node_mass(key, part):
    key_flip = jax.random.fold_in(key, 201)
    key_elem = jax.random.fold_in(key, 203)
    key_node = jax.random.fold_in(key, 205)
    flip = jax.random.randint(key_flip, (), 0, 2)
    rows_idx = jnp.arange(NEX, dtype=jnp.int32)[:, None]
    cols_idx = jnp.arange(NEY, dtype=jnp.int32)[None, :]
    heavy = (rows_idx + cols_idx + flip) % 2 == 0
    spread = jax.random.uniform(key_elem, (NEX, NEY), jnp.float32, 0.0, 1.0)
    heavy_vals = 2.0 * jnp.exp(math.log(2.0) * spread)
    light_vals = 0.1 * jnp.exp(math.log(2.0) * spread)
    element_mass = jnp.where(heavy, heavy_vals, light_vals)
    expanded = jnp.repeat(jnp.repeat(element_mass, 4, axis=0), 4, axis=1)
    jitter = jnp.exp(jax.random.uniform(key_node, (4 * NEX, 4 * NEY), jnp.float32, math.log(0.7), math.log(1.4)))
    return (expanded * jitter).astype(jnp.float32)


def shard_levels(rng, extent, pieces, smallest, largest):
    factor_of = 1.0
    for dim, parts in pieces:
        steps = jax.random.uniform(jax.random.fold_in(jax.random.fold_in(rng, 6), dim), (parts,), jnp.float32, smallest / len(pieces), largest / len(pieces))
        factor_of = factor_of * jnp.repeat(jnp.exp(steps), extent[dim] // parts).reshape((-1,) + (1,) * (len(extent) - 1 - dim))
    return factor_of


def centred(own_key, dims, width, reach, shards=(), kind=jnp.bfloat16):
    level = shard_levels(own_key, dims, shards, -0.22, 0.18) if shards else 1.0
    values = jax.random.normal(own_key, dims, jnp.float32) * width * level
    return jnp.minimum(jnp.maximum(values, -reach), reach).astype(kind)


def setup_inputs(seed: int = 0) -> dict:
    keys = jax.random.split(jax.random.key(seed), 7)
    return {
        "tracers": centred(keys[0], (2, LEV, 4 * NEX, 4 * NEY), 1.0, 6.0, ((2, 16), (3, 64)), jnp.float32),
        "winds": draw_winds(jax.random.fold_in(keys[6], 71), 0),
        "node_mass": draw_node_mass(jax.random.fold_in(keys[6], 71), 0),
        "column_cost": draw_column_cost(jax.random.fold_in(keys[6], 71), 0),
        "weight_in": centred(keys[4], (4 * LEV, HID), (4 * LEV) ** -0.5, 0.375),
        "weight_out": centred(keys[5], (HID, 4 * LEV), HID ** -0.5, 0.1875),
    }


time_step = 0.02
remap_table = ((0.45, 0.4, 0.15, 0.0), (0.0, 0.15, 0.4, 0.45))
gll_points = (-1.0, -0.4472135954999579, 0.4472135954999579, 1.0)


def gll_matrix():
    matrix = []
    for row_idx in range(4):
        entries = []
        for col_idx in range(4):
            if row_idx == col_idx:
                running = 0.0
                for third_idx in range(4):
                    if third_idx != row_idx:
                        running += 1.0 / (gll_points[row_idx] - gll_points[third_idx])
                entries.append(2.0 * running)
            else:
                numerator = 1.0
                denominator = 1.0
                for third_idx in range(4):
                    if third_idx != row_idx:
                        numerator *= gll_points[row_idx] - gll_points[third_idx]
                    if third_idx != col_idx:
                        denominator *= gll_points[col_idx] - gll_points[third_idx]
                entries.append(2.0 * numerator / (denominator * (gll_points[row_idx] - gll_points[col_idx])))
        matrix.append(entries)
    return matrix


def derivatives(values):
    derivative = jnp.array(gll_matrix(), jnp.float32)
    layout = values.shape
    blocks_x = values.reshape(layout[:-2] + (layout[-2] // 4, 4, layout[-1]))
    along_x = jnp.einsum("ij,...ejy->...eiy", derivative, blocks_x, precision=lax.Precision.HIGHEST).reshape(layout)
    blocks_y = values.reshape(layout[:-1] + (layout[-1] // 4, 4))
    along_y = jnp.einsum("ij,...ej->...ei", derivative, blocks_y, precision=lax.Precision.HIGHEST).reshape(layout)
    return along_x, along_y


def tendency(tracer_vals, wind_vals):
    along_x, along_y = derivatives(tracer_vals)
    speeds = wind_vals.astype(jnp.float32)
    return -(speeds[0] * along_x + speeds[1] * along_y)


def assemble(values):
    layout = values.shape
    blocks = values.reshape(layout[:-2] + (layout[-2] // 4, 4, layout[-1]))
    first_edge = blocks[..., 0, :]
    last_edge = blocks[..., 3, :]
    new_first = first_edge + jnp.roll(last_edge, 1, axis=-2)
    new_last = last_edge + jnp.roll(first_edge, -1, axis=-2)
    blocks = jnp.concatenate([new_first[..., None, :], blocks[..., 1:3, :], new_last[..., None, :]], axis=-2)
    values = blocks.reshape(layout)
    blocks = values.reshape(layout[:-1] + (layout[-1] // 4, 4))
    first_edge = blocks[..., 0]
    last_edge = blocks[..., 3]
    new_first = first_edge + jnp.roll(last_edge, 1, axis=-1)
    new_last = last_edge + jnp.roll(first_edge, -1, axis=-1)
    blocks = jnp.concatenate([new_first[..., None], blocks[..., 1:3], new_last[..., None]], axis=-1)
    return blocks.reshape(layout)


def remap_columns(stacked):
    weights_table = jnp.array(remap_table, jnp.float32)
    layout = stacked.shape
    blocks = stacked.reshape(layout[:-2] + (layout[-2] // 4, 4, layout[-1] // 4, 4))
    cell_values = jnp.einsum("pa,qb,...xayb->...xpyq", weights_table, weights_table, blocks, precision=lax.Precision.HIGHEST)
    return cell_values.reshape(layout[:-2] + (layout[-2] // 2, layout[-1] // 2))


def network_step(column_state, weight_in, weight_out):
    hidden = jax.nn.gelu(jnp.dot(column_state.astype(jnp.bfloat16), weight_in, preferred_element_type=jnp.float32)).astype(jnp.bfloat16)
    return column_state + jnp.dot(hidden, weight_out, preferred_element_type=jnp.float32)


def blockwise(block_rows, weight_in, weight_out):
    blocks_count = block_rows.shape[0] // COLS
    mapped = lax.map(lambda one_block: network_step(one_block, weight_in, weight_out), block_rows.reshape(blocks_count, COLS, block_rows.shape[1]))
    return mapped.reshape(block_rows.shape)


def reference(tracers, winds, node_mass, column_cost, weight_in, weight_out):
    assembled = assemble(node_mass)

    def one_level(level_pair):
        tracer_level, wind_level = level_pair
        summed = assemble(tendency(tracer_level, wind_level) * node_mass)
        updated = tracer_level + time_step * (summed / assembled)
        stacked = jnp.concatenate([updated, wind_level.astype(jnp.float32)], axis=0)
        return updated, remap_columns(stacked).astype(jnp.bfloat16)

    by_level = (jnp.moveaxis(tracers, 1, 0), jnp.moveaxis(winds, 1, 0))
    updated, cell_values = lax.map(one_level, by_level)
    tracers_next = jnp.moveaxis(updated, 0, 1)
    cell_values = jnp.moveaxis(cell_values, 0, 1)
    features = cell_values.shape[0] * cell_values.shape[1]
    column_state = cell_values.reshape(features, -1).T.astype(jnp.float32)
    flat_cost = column_cost.reshape(-1)
    sorted_order = jnp.argsort(3 - flat_cost, stable=True)
    inverse = jnp.argsort(sorted_order, stable=True)
    column_state = column_state[sorted_order]
    everything = column_state.shape[0]
    for fraction in (1, 2, 4):
        leading = everything // fraction
        column_state = jnp.concatenate([blockwise(column_state[:leading], weight_in, weight_out), column_state[leading:]], axis=0)
    column_state = column_state[inverse].astype(jnp.bfloat16)
    columns_out = column_state.T.reshape(cell_values.shape)
    return tracers_next, columns_out
```

```python
import functools

import jax
import jax.numpy as jnp
import ml_dtypes
import numpy as np
from jax import lax
from jax.experimental import pallas as pl
from jax.experimental.pallas import tpu as pltpu
from jax.sharding import PartitionSpec as P

time_step = 0.02
remap_table = ((0.45, 0.4, 0.15, 0.0), (0.0, 0.15, 0.4, 0.45))
gll_points = (-1.0, -0.4472135954999579, 0.4472135954999579, 1.0)
f32, bf16 = jnp.float32, jnp.bfloat16
CHUNK = 16
ROWS = 144
NT = (((1,), (1,)), ((), ()))


def gll_matrix():
    matrix = []
    for row_idx in range(4):
        entries = []
        for col_idx in range(4):
            if row_idx == col_idx:
                running = 0.0
                for third_idx in range(4):
                    if third_idx != row_idx:
                        running += 1.0 / (gll_points[row_idx] - gll_points[third_idx])
                entries.append(2.0 * running)
            else:
                numerator = 1.0
                denominator = 1.0
                for third_idx in range(4):
                    if third_idx != row_idx:
                        numerator *= gll_points[row_idx] - gll_points[third_idx]
                    if third_idx != col_idx:
                        denominator *= gll_points[col_idx] - gll_points[third_idx]
                entries.append(
                    2.0 * numerator / (denominator * (gll_points[row_idx] - gll_points[col_idx]))
                )
        matrix.append(entries)
    return matrix


def split_bf16(values):
    high = values.astype(np.float32).astype(ml_dtypes.bfloat16)
    low = (values.astype(np.float32) - high.astype(np.float32)).astype(ml_dtypes.bfloat16)
    return high, low


def lane_derivative():
    block = np.kron(np.eye(32), np.array(gll_matrix()).T)
    high, low = split_bf16(block)
    return np.block([[high, low], [high, np.zeros_like(low)]])


def lane_remap():
    high, low = split_bf16(np.kron(np.eye(64), np.array(remap_table)))
    return np.concatenate([high, low], axis=0)


def lane_index(shape):
    return lax.broadcasted_iota(jnp.int32, shape, 1)


def assemble_lanes(values):
    lane = lane_index(values.shape)
    inside = lane % 4
    first = jnp.logical_and(inside == 0, lane > 0)
    last = jnp.logical_and(inside == 3, lane < values.shape[1] - 1)
    return (
        values
        + jnp.where(first, pltpu.roll(values, 1, 1), 0.0)
        + jnp.where(last, pltpu.roll(values, values.shape[1] - 1, 1), 0.0)
    )


def edge_columns(planes):
    lane = lane_index((planes[0].shape[0], 128))
    left = jnp.zeros(lane.shape, f32)
    right = jnp.zeros(lane.shape, f32)
    for a in range(4):
        low, high = planes[a][:, :128], planes[a][:, 128:]
        left = jnp.where(lane == a, pltpu.roll(low, a, 1) if a else low, left)
        right = jnp.where(lane == 124 + a, pltpu.roll(high, 125 + a, 1) if a < 3 else high, right)
    return left, right


def tendency_kernel(t_ref, w_ref, m_ref, dy_ref, g_ref, gm_ref, up_ref, dn_ref, left_ref, right_ref, wf_ref):
    derivative = gll_matrix()
    mass = m_ref[...]
    wf_ref[...] = w_ref[...].astype(f32)
    mass_rows = assemble_lanes(jnp.concatenate([mass[0:4], mass[4:8]], axis=1))
    gm_ref[...] = mass_rows
    pad = jnp.zeros((ROWS - 129, 256), f32)
    up_ref[128:, :] = jnp.concatenate([mass_rows[3:4], pad], axis=0).astype(bf16)
    dn_ref[128:, :] = jnp.concatenate([mass_rows[0:1], pad], axis=0).astype(bf16)
    row_left, row_right = edge_columns([mass_rows[a : a + 1] for a in range(4)])
    pad = jnp.zeros((ROWS - 129, 128), f32)
    left_ref[128:, :] = jnp.concatenate([row_left, pad], axis=0)
    right_ref[128:, :] = jnp.concatenate([row_right, pad], axis=0)
    for k in range(2):
        for group in range(64 // CHUNK):
            level = group * CHUNK
            channel = k * 64 + level
            places = [(a, j) for a in range(4) for j in range(2)]
            x = {
                (a, j): t_ref[pl.ds(channel * 8 + j * 4 + a, CHUNK, stride=8), :]
                for a, j in places
            }
            lhs = []
            for place in places:
                high = x[place].astype(bf16)
                low = (x[place] - high.astype(f32)).astype(bf16)
                lhs.append(jnp.concatenate([high, low], axis=1))
            product = jnp.dot(
                jnp.concatenate(lhs, axis=0), dy_ref[...], preferred_element_type=f32
            )
            along_y = product[:, :128] + product[:, 128:]
            planes = []
            for a in range(4):
                halves = []
                for j in range(2):
                    along_x = derivative[a][0] * x[0, j]
                    for b in range(1, 4):
                        along_x += derivative[a][b] * x[b, j]
                    position = places.index((a, j)) * CHUNK
                    u = wf_ref[pl.ds(level * 8 + j * 4 + a, CHUNK, stride=8), :]
                    v = wf_ref[pl.ds(512 + level * 8 + j * 4 + a, CHUNK, stride=8), :]
                    total = u * along_x + v * along_y[position : position + CHUNK]
                    halves.append(-total * mass[j * 4 + a : j * 4 + a + 1, :])
                plane = assemble_lanes(jnp.concatenate(halves, axis=1))
                g_ref[a, channel : channel + CHUNK, :] = plane
                planes.append(plane)
            up_ref[channel : channel + CHUNK, :] = planes[3].astype(bf16)
            dn_ref[channel : channel + CHUNK, :] = planes[0].astype(bf16)
            left, right = edge_columns(planes)
            left_ref[channel : channel + CHUNK, :] = left
            right_ref[channel : channel + CHUNK, :] = right


def beside_kernel(w_ref, cost_ref, rt_ref, cells_ref, costs_ref, wf_ref, planes_ref):
    wf_ref[...] = w_ref[...].astype(f32)
    for k in range(2):
        for group in range(64 // CHUNK):
            channel = k * 64 + group * CHUNK
            sums = [None, None]
            for a in range(4):
                row = jnp.concatenate(
                    [
                        wf_ref[pl.ds(channel * 8 + j * 4 + a, CHUNK, stride=8), :]
                        for j in range(2)
                    ],
                    axis=1,
                )
                for p in range(2):
                    if remap_table[p][a]:
                        term = remap_table[p][a] * row
                        sums[p] = term if sums[p] is None else sums[p] + term
            for p in range(2):
                planes_ref[p, channel : channel + CHUNK, :] = sums[p].astype(bf16)
    eye = lax.broadcasted_iota(jnp.int32, (128, 128), 0) == lane_index((128, 128))
    for p in range(2):
        product = lax.dot_general(rt_ref[...], planes_ref[p], NT, preferred_element_type=f32)
        cells_ref[p * 128 : (p + 1) * 128, :] = (product[:128] + product[128:]).astype(bf16)
        diagonal = jnp.where(eye, cost_ref[p : p + 1, :].astype(f32), 0.0).astype(bf16)
        costs_ref[p * 128 : (p + 1) * 128, :] = jnp.dot(
            diagonal, jnp.ones((128, 128), bf16), preferred_element_type=f32
        )


def edges_kernel(left_ref, right_ref, r0_ref, r3_ref, to_left_ref, to_right_ref):
    lane = lane_index((ROWS, 128))
    r0 = r0_ref[...].astype(f32)
    r3 = r3_ref[...].astype(f32)
    left = left_ref[...] + jnp.where(lane == 0, r0[:, :128], 0.0)
    left += jnp.where(lane == 3, pltpu.roll(r3[:, :128], 3, 1), 0.0)
    right = right_ref[...] + jnp.where(lane == 127, r3[:, 128:], 0.0)
    right += jnp.where(lane == 124, pltpu.roll(r0[:, 128:], 125, 1), 0.0)
    to_left_ref[...] = left.astype(bf16)
    to_right_ref[...] = right.astype(bf16)


def gelu(x):
    inner = x * (0.7978845608028654 + 0.035677408136300125 * (x * x))
    half = 0.5 * x
    return half + half * jnp.tanh(inner)


def finish_kernel(
    t_ref, g_ref, gm_ref, r0_ref, r3_ref, cl_ref, cr_ref, cells_ref, costs_ref, rt_ref, wi_ref, wo_ref,
    t_out, c_out, planes_ref, turned_ref,
):
    def complete(a, own, start, size):
        if a == 0:
            own += r0_ref[start : start + 16, :].astype(f32)[:size]
        if a == 3:
            own += r3_ref[start : start + 16, :].astype(f32)[:size]
        lane = lane_index((size, 128))
        left = cl_ref[start : start + 16, :].astype(f32)[:size]
        right = cr_ref[start : start + 16, :].astype(f32)[:size]
        left = jnp.where(lane == 0, pltpu.roll(left, 4 - a, 1), 0.0)
        right = jnp.where(lane == 127, pltpu.roll(right, 127 - a, 1), 0.0)
        return jnp.concatenate([own[:, :128] + left, own[:, 128:] + right], axis=1)

    scale = [time_step / complete(a, gm_ref[a : a + 1, :], 128, 1) for a in range(4)]
    for channel in range(0, 128, CHUNK):
        sums = [None, None]
        for a in range(4):
            step = complete(a, g_ref[a, channel : channel + CHUNK, :], channel, CHUNK) * scale[a]
            halves = []
            for j in range(2):
                rows = pl.ds(channel * 8 + j * 4 + a, CHUNK, stride=8)
                value = t_ref[rows, :] + step[:, j * 128 : (j + 1) * 128]
                t_out[rows, :] = value
                halves.append(value)
            row = jnp.concatenate(halves, axis=1)
            for p in range(2):
                if remap_table[p][a]:
                    term = remap_table[p][a] * row
                    sums[p] = term if sums[p] is None else sums[p] + term
        for p in range(2):
            planes_ref[p, channel : channel + CHUNK, :] = sums[p].astype(bf16)
    states = []
    for p in range(2):
        product = lax.dot_general(rt_ref[...], planes_ref[p], NT, preferred_element_type=f32)
        tracer_cells = (product[:128] + product[128:]).astype(bf16).astype(f32)
        wind_cells = cells_ref[p * 128 : (p + 1) * 128, :].astype(f32)
        states.append(jnp.concatenate([tracer_cells, wind_cells], axis=1))
    state = jnp.concatenate(states, axis=0)
    costs = jnp.concatenate([costs_ref[...], costs_ref[...]], axis=1)
    for substep in range(3):
        rounded = state.astype(bf16)
        stepped = state
        for h in range(0, 1024, 256):
            hidden = jnp.dot(rounded, wi_ref[:, h : h + 256], preferred_element_type=f32)
            stepped += jnp.dot(
                gelu(hidden).astype(bf16), wo_ref[h : h + 256, :], preferred_element_type=f32
            )
        state = jnp.where(costs > substep, stepped, state)
    rounded = state.astype(bf16)
    eye = lax.broadcasted_iota(jnp.int32, (256, 256), 0) == lane_index((256, 256))
    eye = jnp.where(eye, 1.0, 0.0).astype(bf16)
    for p in range(2):
        turned_ref[pl.ds(p, 256, stride=2), :] = lax.dot_general(
            eye, rounded[p * 128 : (p + 1) * 128], NT, preferred_element_type=f32
        )
    c_out[...] = turned_ref[...].astype(bf16)


def call(kernel, outs, scratch, name):
    vmem = pl.BlockSpec(memory_space=pltpu.VMEM)
    shapes = tuple(jax.ShapeDtypeStruct(*o) for o in outs)

    def run(*args):
        return pl.pallas_call(
            kernel,
            out_shape=shapes,
            in_specs=[vmem] * len(args),
            out_specs=tuple(vmem for _ in outs),
            scratch_shapes=[pltpu.VMEM(*s) for s in scratch],
            compiler_params=pltpu.CompilerParams(vmem_limit_bytes=24 * 1024 * 1024),
            name=name,
        )(*args)

    return run


def node_rows(array):
    k, levels = array.shape[:2]
    return array.reshape(k, levels, 4, 2, 128).transpose(0, 1, 3, 2, 4).reshape(k * levels * 8, 128)


def shift(value, axis, by):
    count = lax.axis_size(axis)
    return lax.ppermute(value, axis, [(i, (i + by) % count) for i in range(count)])


def shards(tracers, winds, node_mass, column_cost, weight_in, weight_out):
    t = node_rows(tracers)
    w = node_rows(winds)
    m = node_mass.reshape(4, 2, 128).transpose(1, 0, 2).reshape(8, 128)
    g, gm, up, dn, left, right = call(
        tendency_kernel,
        [((4, 128, 256), f32), ((4, 256), f32), ((ROWS, 256), bf16), ((ROWS, 256), bf16), ((ROWS, 128), f32), ((ROWS, 128), f32)],
        [((1024, 128), f32)],
        "tendency",
    )(t, w, m, jnp.asarray(lane_derivative()))
    r0 = shift(up, "grp", 1)
    r3 = shift(dn, "grp", -1)
    remap = jnp.asarray(lane_remap())
    cells, costs = call(
        beside_kernel,
        [((256, 128), bf16), ((256, 128), f32)],
        [((1024, 128), f32), ((2, 128, 256), bf16)],
        "winds",
    )(w, column_cost, remap)
    to_left, to_right = call(
        edges_kernel, [((ROWS, 128), bf16), ((ROWS, 128), bf16)], [], "edges"
    )(left, right, r0, r3)
    cl = shift(to_right, "bal", 1)
    cr = shift(to_left, "bal", -1)
    t_next, columns = call(
        finish_kernel,
        [((1024, 128), f32), ((512, 128), bf16)],
        [((2, 128, 256), bf16), ((512, 128), f32)],
        "finish",
    )(t, g, gm, r0, r3, cl, cr, cells, costs, remap, weight_in, weight_out)
    t_next = t_next.reshape(2, 64, 2, 4, 128).transpose(0, 1, 3, 2, 4).reshape(2, 64, 4, 256)
    return t_next, columns.reshape(4, 64, 2, 128)


def solution(mesh):
    placed = (
        P(None, None, "grp", "bal"),
        P(None, None, "grp", "bal"),
        P("grp", "bal"),
        P("grp", "bal"),
        P(),
        P(),
    )
    return jax.shard_map(
        shards,
        mesh=mesh,
        in_specs=placed,
        out_specs=(P(None, None, "grp", "bal"), P(None, None, "grp", "bal")),
        check_vma=False,
    )
```

```python
import functools

import jax
import jax.numpy as jnp
import ml_dtypes
import numpy as np
from jax import lax
from jax.experimental import pallas as pl
from jax.experimental.pallas import tpu as pltpu
from jax.sharding import PartitionSpec as P

time_step = 0.02
remap_table = ((0.45, 0.4, 0.15, 0.0), (0.0, 0.15, 0.4, 0.45))
gll_points = (-1.0, -0.4472135954999579, 0.4472135954999579, 1.0)
f32, bf16 = jnp.float32, jnp.bfloat16
CHUNK = 16
ROWS = 144
NT = (((1,), (1,)), ((), ()))


def gll_matrix():
    matrix = []
    for row_idx in range(4):
        entries = []
        for col_idx in range(4):
            if row_idx == col_idx:
                running = 0.0
                for third_idx in range(4):
                    if third_idx != row_idx:
                        running += 1.0 / (gll_points[row_idx] - gll_points[third_idx])
                entries.append(2.0 * running)
            else:
                numerator = 1.0
                denominator = 1.0
                for third_idx in range(4):
                    if third_idx != row_idx:
                        numerator *= gll_points[row_idx] - gll_points[third_idx]
                    if third_idx != col_idx:
                        denominator *= gll_points[col_idx] - gll_points[third_idx]
                entries.append(
                    2.0 * numerator / (denominator * (gll_points[row_idx] - gll_points[col_idx]))
                )
        matrix.append(entries)
    return matrix


def split_bf16(values):
    high = values.astype(np.float32).astype(ml_dtypes.bfloat16)
    low = (values.astype(np.float32) - high.astype(np.float32)).astype(ml_dtypes.bfloat16)
    return high, low


def lane_derivative():
    block = np.kron(np.eye(32), np.array(gll_matrix()).T)
    high, low = split_bf16(block)
    return np.block([[high, low], [high, np.zeros_like(low)]])


def lane_remap():
    high, low = split_bf16(np.kron(np.eye(64), np.array(remap_table)))
    return np.concatenate([high, low], axis=0)


def lane_index(shape):
    return lax.broadcasted_iota(jnp.int32, shape, 1)


def assemble_lanes(values):
    lane = lane_index(values.shape)
    inside = lane % 4
    first = jnp.logical_and(inside == 0, lane > 0)
    last = jnp.logical_and(inside == 3, lane < values.shape[1] - 1)
    return (
        values
        + jnp.where(first, pltpu.roll(values, 1, 1), 0.0)
        + jnp.where(last, pltpu.roll(values, values.shape[1] - 1, 1), 0.0)
    )


def edge_columns(planes):
    lane = lane_index((planes[0].shape[0], 128))
    left = jnp.zeros(lane.shape, f32)
    right = jnp.zeros(lane.shape, f32)
    for a in range(4):
        low, high = planes[a][:, :128], planes[a][:, 128:]
        left = jnp.where(lane == a, pltpu.roll(low, a, 1) if a else low, left)
        right = jnp.where(lane == 124 + a, pltpu.roll(high, 125 + a, 1) if a < 3 else high, right)
    return left, right


def row_of(a):
    odd = lax.axis_index("grp") % 2
    return a + odd * (3 - 2 * a)


def weighted_rows(rows, channel, t_ref, wf_ref, mass, dy_ref):
    derivative = gll_matrix()
    sign = jnp.where(lax.axis_index("grp") % 2 == 1, -1.0, 1.0)
    level = channel % 64
    x = {
        (a, j): t_ref[pl.ds(channel * 8 + j * 4 + row_of(a), CHUNK, stride=8), :]
        for a in range(4)
        for j in range(2)
    }
    lhs = []
    for a in rows:
        for j in range(2):
            high = x[a, j].astype(bf16)
            low = (x[a, j] - high.astype(f32)).astype(bf16)
            lhs.append(jnp.concatenate([high, low], axis=1))
    product = jnp.dot(jnp.concatenate(lhs, axis=0), dy_ref[...], preferred_element_type=f32)
    along_y = product[:, :128] + product[:, 128:]
    planes = []
    for n, a in enumerate(rows):
        halves = []
        for j in range(2):
            along_x = derivative[a][0] * x[0, j]
            for b in range(1, 4):
                along_x += derivative[a][b] * x[b, j]
            position = (2 * n + j) * CHUNK
            u = wf_ref[pl.ds(level * 8 + j * 4 + row_of(a), CHUNK, stride=8), :]
            v = wf_ref[pl.ds(512 + level * 8 + j * 4 + row_of(a), CHUNK, stride=8), :]
            total = (sign * u) * along_x + v * along_y[position : position + CHUNK]
            halves.append(-total * mass[j * 4 + a : j * 4 + a + 1, :])
        planes.append(assemble_lanes(jnp.concatenate(halves, axis=1)))
    return planes


def tendency_kernel(
    t_hbm, w_hbm, m_hbm, dy_hbm, t_ref, wf_ref, mass_ref, dy_ref, g_ref, gm_ref, outer_ref, inner_ref,
    w_ref, m_ref, sems,
):
    copies = [
        pltpu.make_async_copy(source, target, sems.at[i])
        for i, (source, target) in enumerate(
            [(w_hbm, w_ref), (t_hbm, t_ref), (m_hbm, m_ref), (dy_hbm, dy_ref)]
        )
    ]
    for copy in copies:
        copy.start()
    for copy in copies:
        copy.wait()
    mass = m_ref[...]
    backward = jnp.concatenate([mass[i : i + 1] for i in (3, 2, 1, 0, 7, 6, 5, 4)], axis=0)
    mass = jnp.where(lax.axis_index("grp") % 2 == 1, backward, mass)
    mass_ref[...] = mass
    wf_ref[...] = w_ref[...].astype(f32)
    mass_rows = assemble_lanes(jnp.concatenate([mass[0:4], mass[4:8]], axis=1))
    gm_ref[...] = mass_rows
    pad = jnp.zeros((ROWS - 129, 256), f32)
    outer_ref[128:, :] = jnp.concatenate([mass_rows[0:1], pad], axis=0).astype(bf16)
    inner_ref[128:, :] = jnp.concatenate([mass_rows[3:4], pad], axis=0).astype(bf16)
    for channel in range(0, 128, CHUNK):
        rows = slice(channel, channel + CHUNK)
        planes = weighted_rows((0, 3), channel, t_ref, wf_ref, mass, dy_ref)
        for n, target in enumerate((outer_ref, inner_ref)):
            g_ref[n, rows, :] = planes[n]
            target[rows, :] = planes[n].astype(bf16)


def middle_kernel(t_ref, wf_ref, mass_ref, dy_ref, gm_ref, ends_ref, g_ref, left_ref, right_ref):
    mass = mass_ref[...]
    row_left, row_right = edge_columns([gm_ref[a : a + 1, :] for a in range(4)])
    pad = jnp.zeros((ROWS - 129, 128), f32)
    left_ref[128:, :] = jnp.concatenate([row_left, pad], axis=0)
    right_ref[128:, :] = jnp.concatenate([row_right, pad], axis=0)
    for channel in range(0, 128, CHUNK):
        rows = slice(channel, channel + CHUNK)
        planes = weighted_rows((1, 2), channel, t_ref, wf_ref, mass, dy_ref)
        for n in range(2):
            g_ref[n, rows, :] = planes[n]
        left, right = edge_columns([ends_ref[0, rows, :], *planes, ends_ref[1, rows, :]])
        left_ref[rows, :] = left
        right_ref[rows, :] = right


def beside_kernel(
    wf_ref, cost_ref, rt_ref, wi_hbm, wo_hbm, after_ref, cells_ref, costs_ref, wi_ref, wo_ref, planes_ref, sems
):
    first = pltpu.make_async_copy(wi_hbm, wi_ref, sems.at[0])
    second = pltpu.make_async_copy(wo_hbm, wo_ref, sems.at[1])
    first.start()
    second.start()
    for k in range(2):
        for group in range(64 // CHUNK):
            channel = k * 64 + group * CHUNK
            sums = [None, None]
            for a in range(4):
                row = jnp.concatenate(
                    [
                        wf_ref[pl.ds(channel * 8 + j * 4 + a, CHUNK, stride=8), :]
                        for j in range(2)
                    ],
                    axis=1,
                )
                for p in range(2):
                    if remap_table[p][a]:
                        term = remap_table[p][a] * row
                        sums[p] = term if sums[p] is None else sums[p] + term
            for p in range(2):
                planes_ref[p, channel : channel + CHUNK, :] = sums[p].astype(bf16)
    eye = lax.broadcasted_iota(jnp.int32, (128, 128), 0) == lane_index((128, 128))
    for p in range(2):
        product = lax.dot_general(rt_ref[...], planes_ref[p], NT, preferred_element_type=f32)
        cells_ref[p * 128 : (p + 1) * 128, :] = (product[:128] + product[128:]).astype(bf16)
        diagonal = jnp.where(eye, cost_ref[p : p + 1, :].astype(f32), 0.0).astype(bf16)
        costs_ref[p * 128 : (p + 1) * 128, :] = jnp.dot(
            diagonal, jnp.ones((128, 128), bf16), preferred_element_type=f32
        )
    first.wait()
    second.wait()


def with_columns(a, own, cl, cr):
    lane = lane_index(cl.shape)
    left = jnp.where(lane == 0, pltpu.roll(cl, 4 - a, 1), 0.0)
    right = jnp.where(lane == 127, pltpu.roll(cr, 127 - a, 1), 0.0)
    return jnp.concatenate([own[:, :128] + left, own[:, 128:] + right], axis=1)


def edges_kernel(left_ref, right_ref, r0_ref, r3_ref, to_left_ref, to_right_ref):
    lane = lane_index((ROWS, 128))
    r0 = r0_ref[...].astype(f32)
    r3 = r3_ref[...].astype(f32)
    left = left_ref[...] + jnp.where(lane == 0, r0[:, :128], 0.0)
    left += jnp.where(lane == 3, pltpu.roll(r3[:, :128], 3, 1), 0.0)
    right = right_ref[...] + jnp.where(lane == 127, r3[:, 128:], 0.0)
    right += jnp.where(lane == 124, pltpu.roll(r0[:, 128:], 125, 1), 0.0)
    to_left_ref[...] = left.astype(bf16)
    to_right_ref[...] = right.astype(bf16)


def gelu(x):
    inner = x * (0.7978845608028654 + 0.035677408136300125 * (x * x))
    half = 0.5 * x
    return half + half * jnp.tanh(inner)


def cell_row(p):
    odd = lax.axis_index("grp") % 2
    return p + odd * (1 - 2 * p)


def finish_kernel(
    t_ref, ends_ref, middle_ref, gm_ref, r0_ref, r3_ref, cl_ref, cr_ref, cells_ref, costs_ref, rt_ref, wi_ref, wo_ref,
    t_hbm, c_hbm, planes_ref, turned_ref, t_out, c_out, sems,
):
    def complete(a, own, start, size):
        rows = slice(start, start + CHUNK)
        if a in (0, 3):
            own += (r0_ref if a == 0 else r3_ref)[rows, :].astype(f32)[:size]
        return with_columns(a, own, cl_ref[rows, :].astype(f32)[:size], cr_ref[rows, :].astype(f32)[:size])

    scale = [time_step / complete(a, gm_ref[a : a + 1, :], 128, 1) for a in range(4)]
    for channel in range(0, 128, CHUNK):
        sums = [None, None]
        for a in range(4):
            source, n = (ends_ref, a // 3) if a in (0, 3) else (middle_ref, a - 1)
            change = complete(a, source[n, channel : channel + CHUNK, :], channel, CHUNK) * scale[a]
            halves = []
            for j in range(2):
                rows = pl.ds(channel * 8 + j * 4 + row_of(a), CHUNK, stride=8)
                value = t_ref[rows, :] + change[:, j * 128 : (j + 1) * 128]
                t_out[rows, :] = value
                halves.append(value)
            row = jnp.concatenate(halves, axis=1)
            for p in range(2):
                if remap_table[p][a]:
                    term = remap_table[p][a] * row
                    sums[p] = term if sums[p] is None else sums[p] + term
        for p in range(2):
            planes_ref[p, channel : channel + CHUNK, :] = sums[p].astype(bf16)
    store = pltpu.make_async_copy(t_out, t_hbm, sems.at[0])
    store.start()
    states, costs = [], []
    for p in range(2):
        product = lax.dot_general(rt_ref[...], planes_ref[p], NT, preferred_element_type=f32)
        tracer_cells = (product[:128] + product[128:]).astype(bf16).astype(f32)
        own = pl.ds(pl.multiple_of(cell_row(p) * 128, 128), 128)
        states.append(jnp.concatenate([tracer_cells, cells_ref[own, :].astype(f32)], axis=1))
        costs.append(jnp.concatenate([costs_ref[own, :], costs_ref[own, :]], axis=1))
    for substep in range(3):
        for p in range(2):
            rounded = states[p].astype(bf16)
            stepped = states[p]
            for h in range(0, 1024, 256):
                hidden = jnp.dot(rounded, wi_ref[:, h : h + 256], preferred_element_type=f32)
                stepped += jnp.dot(
                    gelu(hidden).astype(bf16), wo_ref[h : h + 256, :], preferred_element_type=f32
                )
            states[p] = jnp.where(costs[p] > substep, stepped, states[p])
    eye = lax.broadcasted_iota(jnp.int32, (256, 256), 0) == lane_index((256, 256))
    eye = jnp.where(eye, 1.0, 0.0).astype(bf16)
    for p in range(2):
        turned_ref[pl.ds(cell_row(p), 256, stride=2), :] = lax.dot_general(
            eye, states[p].astype(bf16), NT, preferred_element_type=f32
        )
    c_out[...] = turned_ref[...].astype(bf16)
    final = pltpu.make_async_copy(c_out, c_hbm, sems.at[1])
    final.start()
    store.wait()
    final.wait()


def call(kernel, outs, scratch, name, hbm_in=(), hbm_out=(), semaphores=0):
    shapes = tuple(jax.ShapeDtypeStruct(*o) for o in outs)
    scratch = [pltpu.VMEM(*s) for s in scratch]
    if semaphores:
        scratch.append(pltpu.SemaphoreType.DMA((semaphores,)))

    def spec(in_hbm):
        return pl.BlockSpec(memory_space=pltpu.HBM if in_hbm else pltpu.VMEM)

    def run(*args):
        args = [
            pltpu.with_memory_space_constraint(x, pltpu.HBM) if i in hbm_in else x
            for i, x in enumerate(args)
        ]
        return pl.pallas_call(
            kernel,
            out_shape=shapes,
            in_specs=[spec(i in hbm_in) for i in range(len(args))],
            out_specs=tuple(spec(i in hbm_out) for i in range(len(outs))),
            scratch_shapes=scratch,
            compiler_params=pltpu.CompilerParams(vmem_limit_bytes=24 * 1024 * 1024),
            name=name,
        )(*args)

    return run


def node_rows(array):
    k, levels = array.shape[:2]
    return array.reshape(k, levels, 4, 2, 128).transpose(0, 1, 3, 2, 4).reshape(k * levels * 8, 128)


def shift(value, axis, by):
    count = lax.axis_size(axis)
    return lax.ppermute(value, axis, [(i, (i + by) % count) for i in range(count)])


def shards(tracers, winds, node_mass, column_cost, weight_in, weight_out):
    t = node_rows(tracers)
    w = node_rows(winds)
    m = node_mass.reshape(4, 2, 128).transpose(1, 0, 2).reshape(8, 128)
    column, message = ((ROWS, 128), f32), ((ROWS, 256), bf16)
    pair, nodes = ((2, 128, 256), f32), ((1024, 128), f32)
    t, wf, mass, dy, ends, gm, outer, inner = call(
        tendency_kernel,
        [nodes, nodes, ((8, 128), f32), ((256, 256), bf16), pair, ((4, 256), f32), message, message],
        [((1024, 128), bf16), ((8, 128), f32)],
        "tendency",
        hbm_in=(0, 1, 2, 3),
        semaphores=4,
    )(t, w, m, jnp.asarray(lane_derivative()))
    middle, left, right = call(middle_kernel, [pair, column, column], [], "middle")(
        t, wf, mass, dy, gm, ends
    )
    count = lax.axis_size("grp")
    r0 = lax.ppermute(outer, "grp", [(i, (i + (1 if i % 2 else -1)) % count) for i in range(count)])
    r3 = lax.ppermute(inner, "grp", [(i, i ^ 1) for i in range(count)])
    column = ((ROWS, 128), bf16)
    to_left, to_right = call(edges_kernel, [column, column], [], "edges")(left, right, r0, r3)
    cl = shift(to_right, "bal", 1)
    cr = shift(to_left, "bal", -1)
    remap = jnp.asarray(lane_remap())
    cells, costs, first_weights, second_weights = call(
        beside_kernel,
        [((256, 128), bf16), ((256, 128), f32), ((256, 1024), bf16), ((1024, 256), bf16)],
        [((2, 128, 256), bf16)],
        "winds",
        hbm_in=(3, 4),
        semaphores=2,
    )(wf, column_cost, remap, weight_in, weight_out, to_left)
    t_next, columns = call(
        finish_kernel,
        [((1024, 128), f32), ((512, 128), bf16)],
        [((2, 128, 256), bf16), ((512, 128), f32), ((1024, 128), f32), ((512, 128), bf16)],
        "finish",
        hbm_out=(0, 1),
        semaphores=2,
    )(t, ends, middle, gm, r0, r3, cl, cr, cells, costs, remap, first_weights, second_weights)
    t_next = t_next.reshape(2, 64, 2, 4, 128).transpose(0, 1, 3, 2, 4).reshape(2, 64, 4, 256)
    return t_next, columns.reshape(4, 64, 2, 128)


def solution(mesh):
    placed = (
        P(None, None, "grp", "bal"),
        P(None, None, "grp", "bal"),
        P("grp", "bal"),
        P("grp", "bal"),
        P(),
        P(),
    )
    return jax.shard_map(
        shards,
        mesh=mesh,
        in_specs=placed,
        out_specs=(P(None, None, "grp", "bal"), P(None, None, "grp", "bal")),
        check_vma=False,
    )
```

```python
import functools

import jax
import jax.numpy as jnp
import ml_dtypes
import numpy as np
from jax import lax
from jax.experimental import pallas as pl
from jax.experimental.pallas import tpu as pltpu
from jax.sharding import PartitionSpec as P

time_step = 0.02
remap_table = ((0.45, 0.4, 0.15, 0.0), (0.0, 0.15, 0.4, 0.45))
gll_points = (-1.0, -0.4472135954999579, 0.4472135954999579, 1.0)
f32, bf16 = jnp.float32, jnp.bfloat16
CHUNK = 16
ROWS = 144
NT = (((1,), (1,)), ((), ()))


def gll_matrix():
    matrix = []
    for row_idx in range(4):
        entries = []
        for col_idx in range(4):
            if row_idx == col_idx:
                running = 0.0
                for third_idx in range(4):
                    if third_idx != row_idx:
                        running += 1.0 / (gll_points[row_idx] - gll_points[third_idx])
                entries.append(2.0 * running)
            else:
                numerator = 1.0
                denominator = 1.0
                for third_idx in range(4):
                    if third_idx != row_idx:
                        numerator *= gll_points[row_idx] - gll_points[third_idx]
                    if third_idx != col_idx:
                        denominator *= gll_points[col_idx] - gll_points[third_idx]
                entries.append(
                    2.0 * numerator / (denominator * (gll_points[row_idx] - gll_points[col_idx]))
                )
        matrix.append(entries)
    return matrix


def split_bf16(values):
    high = values.astype(np.float32).astype(ml_dtypes.bfloat16)
    low = (values.astype(np.float32) - high.astype(np.float32)).astype(ml_dtypes.bfloat16)
    return high, low


def lane_derivative():
    block = np.kron(np.eye(32), np.array(gll_matrix()).T)
    high, low = split_bf16(block)
    return np.block([[high, low], [high, np.zeros_like(low)]])


def lane_remap():
    high, low = split_bf16(np.kron(np.eye(64), np.array(remap_table)))
    return np.concatenate([high, low], axis=0)


def lane_index(shape):
    return lax.broadcasted_iota(jnp.int32, shape, 1)


def assemble_lanes(values):
    lane = lane_index(values.shape)
    inside = lane % 4
    first = jnp.logical_and(inside == 0, lane > 0)
    last = jnp.logical_and(inside == 3, lane < values.shape[1] - 1)
    return (
        values
        + jnp.where(first, pltpu.roll(values, 1, 1), 0.0)
        + jnp.where(last, pltpu.roll(values, values.shape[1] - 1, 1), 0.0)
    )


def edge_columns(planes):
    lane = lane_index((planes[0].shape[0], 128))
    left = jnp.zeros(lane.shape, f32)
    right = jnp.zeros(lane.shape, f32)
    for a in range(4):
        low, high = planes[a][:, :128], planes[a][:, 128:]
        left = jnp.where(lane == a, pltpu.roll(low, a, 1) if a else low, left)
        right = jnp.where(lane == 124 + a, pltpu.roll(high, 125 + a, 1) if a < 3 else high, right)
    return left, right


def row_of(a):
    odd = lax.axis_index("grp") % 2
    return a + odd * (3 - 2 * a)


def weighted_rows(rows, channel, t_ref, wf_ref, mass, dy_ref):
    derivative = gll_matrix()
    sign = jnp.where(lax.axis_index("grp") % 2 == 1, -1.0, 1.0)
    level = channel % 64
    x = {
        (a, j): t_ref[pl.ds(channel * 8 + j * 4 + row_of(a), CHUNK, stride=8), :]
        for a in range(4)
        for j in range(2)
    }
    lhs = []
    for a in rows:
        for j in range(2):
            high = x[a, j].astype(bf16)
            low = (x[a, j] - high.astype(f32)).astype(bf16)
            lhs.append(jnp.concatenate([high, low], axis=1))
    product = jnp.dot(jnp.concatenate(lhs, axis=0), dy_ref[...], preferred_element_type=f32)
    along_y = product[:, :128] + product[:, 128:]
    planes = []
    for n, a in enumerate(rows):
        halves = []
        for j in range(2):
            along_x = derivative[a][0] * x[0, j]
            for b in range(1, 4):
                along_x += derivative[a][b] * x[b, j]
            position = (2 * n + j) * CHUNK
            u = wf_ref[pl.ds(level * 8 + j * 4 + row_of(a), CHUNK, stride=8), :]
            v = wf_ref[pl.ds(512 + level * 8 + j * 4 + row_of(a), CHUNK, stride=8), :]
            total = (sign * u) * along_x + v * along_y[position : position + CHUNK]
            halves.append(-total * mass[j * 4 + a : j * 4 + a + 1, :])
        planes.append(assemble_lanes(jnp.concatenate(halves, axis=1)))
    return planes


def tendency_kernel(
    t_hbm, w_hbm, m_hbm, dy_hbm, t_ref, wf_ref, mass_ref, dy_ref, g_ref, gm_ref, outer_ref, inner_ref,
    w_ref, m_ref, sems,
):
    copies = [
        pltpu.make_async_copy(source, target, sems.at[i])
        for i, (source, target) in enumerate(
            [(w_hbm, w_ref), (t_hbm, t_ref), (m_hbm, m_ref), (dy_hbm, dy_ref)]
        )
    ]
    for copy in copies:
        copy.start()
    for copy in copies:
        copy.wait()
    mass = m_ref[...]
    backward = jnp.concatenate([mass[i : i + 1] for i in (3, 2, 1, 0, 7, 6, 5, 4)], axis=0)
    mass = jnp.where(lax.axis_index("grp") % 2 == 1, backward, mass)
    mass_ref[...] = mass
    wf_ref[...] = w_ref[...].astype(f32)
    mass_rows = assemble_lanes(jnp.concatenate([mass[0:4], mass[4:8]], axis=1))
    gm_ref[...] = mass_rows
    pad = jnp.zeros((ROWS - 129, 256), f32)
    outer_ref[128:, :] = jnp.concatenate([mass_rows[0:1], pad], axis=0).astype(bf16)
    inner_ref[128:, :] = jnp.concatenate([mass_rows[3:4], pad], axis=0).astype(bf16)
    for channel in range(0, 128, CHUNK):
        rows = slice(channel, channel + CHUNK)
        planes = weighted_rows((0, 3), channel, t_ref, wf_ref, mass, dy_ref)
        for n, target in enumerate((outer_ref, inner_ref)):
            g_ref[n, rows, :] = planes[n]
            target[rows, :] = planes[n].astype(bf16)


def middle_kernel(t_ref, wf_ref, mass_ref, dy_ref, gm_ref, ends_ref, g_ref, left_ref, right_ref):
    mass = mass_ref[...]
    row_left, row_right = edge_columns([gm_ref[a : a + 1, :] for a in range(4)])
    pad = jnp.zeros((ROWS - 129, 128), f32)
    left_ref[128:, :] = jnp.concatenate([row_left, pad], axis=0)
    right_ref[128:, :] = jnp.concatenate([row_right, pad], axis=0)
    for channel in range(0, 128, CHUNK):
        rows = slice(channel, channel + CHUNK)
        planes = weighted_rows((1, 2), channel, t_ref, wf_ref, mass, dy_ref)
        for n in range(2):
            g_ref[n, rows, :] = planes[n]
        left, right = edge_columns([ends_ref[0, rows, :], *planes, ends_ref[1, rows, :]])
        left_ref[rows, :] = left
        right_ref[rows, :] = right


def wind_cells(wf_ref, cost_ref, rt_ref, cells_ref, costs_ref, planes_ref):
    for k in range(2):
        for group in range(64 // CHUNK):
            channel = k * 64 + group * CHUNK
            sums = [None, None]
            for a in range(4):
                row = jnp.concatenate(
                    [wf_ref[pl.ds(channel * 8 + j * 4 + a, CHUNK, stride=8), :] for j in range(2)],
                    axis=1,
                )
                for p in range(2):
                    if remap_table[p][a]:
                        term = remap_table[p][a] * row
                        sums[p] = term if sums[p] is None else sums[p] + term
            for p in range(2):
                planes_ref[p, channel : channel + CHUNK, :] = sums[p].astype(bf16)
    eye = lax.broadcasted_iota(jnp.int32, (128, 128), 0) == lane_index((128, 128))
    for p in range(2):
        product = lax.dot_general(rt_ref[...], planes_ref[p], NT, preferred_element_type=f32)
        cells_ref[p * 128 : (p + 1) * 128, :] = (product[:128] + product[128:]).astype(bf16)
        diagonal = jnp.where(eye, cost_ref[p : p + 1, :].astype(f32), 0.0).astype(bf16)
        costs_ref[p * 128 : (p + 1) * 128, :] = jnp.dot(
            diagonal, jnp.ones((128, 128), bf16), preferred_element_type=f32
        )


def beside_kernel(
    wf_ref, cost_ref, rt_ref, wi_hbm, wo_hbm, after_ref, cells_ref, costs_ref, wi_ref, wo_ref, planes_ref, sems
):
    first = pltpu.make_async_copy(wi_hbm, wi_ref, sems.at[0])
    second = pltpu.make_async_copy(wo_hbm, wo_ref, sems.at[1])
    first.start()
    second.start()
    wind_cells(wf_ref, cost_ref, rt_ref, cells_ref, costs_ref, planes_ref)
    first.wait()
    second.wait()


def with_columns(a, own, cl, cr):
    lane = lane_index(cl.shape)
    left = jnp.where(lane == 0, pltpu.roll(cl, 4 - a, 1), 0.0)
    right = jnp.where(lane == 127, pltpu.roll(cr, 127 - a, 1), 0.0)
    return jnp.concatenate([own[:, :128] + left, own[:, 128:] + right], axis=1)


def edges_kernel(left_ref, right_ref, r0_ref, r3_ref, to_left_ref, to_right_ref):
    lane = lane_index((ROWS, 128))
    r0 = r0_ref[...].astype(f32)
    r3 = r3_ref[...].astype(f32)
    left = left_ref[...] + jnp.where(lane == 0, r0[:, :128], 0.0)
    left += jnp.where(lane == 3, pltpu.roll(r3[:, :128], 3, 1), 0.0)
    right = right_ref[...] + jnp.where(lane == 127, r3[:, 128:], 0.0)
    right += jnp.where(lane == 124, pltpu.roll(r0[:, 128:], 125, 1), 0.0)
    to_left_ref[...] = left.astype(bf16)
    to_right_ref[...] = right.astype(bf16)


def gelu(x):
    inner = x * (0.7978845608028654 + 0.035677408136300125 * (x * x))
    half = 0.5 * x
    return half + half * jnp.tanh(inner)


def cell_row(p):
    odd = lax.axis_index("grp") % 2
    return p + odd * (1 - 2 * p)


def works_early():
    me, last = lax.axis_index("grp"), lax.axis_size("grp") - 1
    return jnp.logical_and(lax.axis_index("bal") == 0, jnp.logical_and(me != 0, me != last))


def move_tracers(t_ref, ends_ref, middle_ref, gm_ref, r0_ref, r3_ref, columns, t_out, planes_ref, edges=None):
    def complete(a, own, start, size):
        rows = slice(start, start + CHUNK)
        if a in (0, 3):
            own += (r0_ref if a == 0 else r3_ref)[rows, :].astype(f32)[:size]
        if columns is None:
            return own
        return with_columns(a, own, *(ref[rows, :].astype(f32)[:size] for ref in columns))

    scale = [time_step / complete(a, gm_ref[a : a + 1, :], 128, 1) for a in range(4)]
    for channel in range(0, 128, CHUNK):
        here = slice(channel, channel + CHUNK)
        sums = [None, None]
        before, after = [], []
        for a in range(4):
            source, n = (ends_ref, a // 3) if a in (0, 3) else (middle_ref, a - 1)
            change = complete(a, source[n, here, :], channel, CHUNK) * scale[a]
            old, new = [], []
            for j in range(2):
                rows = pl.ds(channel * 8 + j * 4 + row_of(a), CHUNK, stride=8)
                old.append(t_ref[rows, :])
                new.append(old[j] + change[:, j * 128 : (j + 1) * 128])
                t_out[rows, :] = new[j]
            row = jnp.concatenate(new, axis=1)
            before.append(jnp.concatenate(old, axis=1))
            after.append(row)
            for p in range(2):
                if remap_table[p][a]:
                    term = remap_table[p][a] * row
                    sums[p] = term if sums[p] is None else sums[p] + term
        for p in range(2):
            planes_ref[p, here, :] = sums[p].astype(bf16)
        if edges is not None:
            for target, values in zip(edges, (*edge_columns(before), *edge_columns(after))):
                target[here, :] = values


def own_cells(p):
    return pl.ds(pl.multiple_of(cell_row(p) * 128, 128), 128)


def entries(p, cells_ref, rt_ref, planes_ref):
    product = lax.dot_general(rt_ref[...], planes_ref[p], NT, preferred_element_type=f32)
    return jnp.concatenate([product[:128] + product[128:], cells_ref[own_cells(p), :].astype(f32)], axis=1)


def network(states, costs, wi_ref, wo_ref):
    states = [state.astype(bf16).astype(f32) for state in states]
    for substep in range(3):
        for p in range(len(states)):
            rounded = states[p].astype(bf16)
            stepped = states[p]
            for h in range(0, 1024, 256):
                hidden = jnp.dot(rounded, wi_ref[:, h : h + 256], preferred_element_type=f32)
                stepped += jnp.dot(
                    gelu(hidden).astype(bf16), wo_ref[h : h + 256, :], preferred_element_type=f32
                )
            states[p] = jnp.where(costs[p] > substep, stepped, states[p])
    return states


def turn(values):
    eye = lax.broadcasted_iota(jnp.int32, (256, 256), 0) == lane_index((256, 256))
    return lax.dot_general(
        jnp.where(eye, 1.0, 0.0).astype(bf16), values.astype(bf16), NT, preferred_element_type=f32
    )


def all_columns(states, costs_ref, wi_ref, wo_ref, turned_ref):
    costs = [jnp.concatenate([costs_ref[own_cells(p), :]] * 2, axis=1) for p in range(2)]
    for p, state in enumerate(network(states, costs, wi_ref, wo_ref)):
        turned_ref[pl.ds(cell_row(p), 256, stride=2), :] = turn(state)


def early_kernel(
    t_ref, ends_ref, middle_ref, gm_ref, r0_ref, r3_ref, wf_ref, cost_hbm, rt_hbm, wi_hbm, wo_hbm,
    t_out, x0_ref, turned_ref, *rest,
):
    *edges, planes_ref, wind_planes_ref, cells_ref, costs_ref, cost_ref, rt_ref, wi_ref, wo_ref, sems = rest

    @pl.when(works_early())
    def _():
        sources, targets = (cost_hbm, rt_hbm, wi_hbm, wo_hbm), (cost_ref, rt_ref, wi_ref, wo_ref)
        copies = [pltpu.make_async_copy(*pair, sems.at[i]) for i, pair in enumerate(zip(sources, targets))]
        for copy in copies:
            copy.start()
        for copy in copies:
            copy.wait()
        wind_cells(wf_ref, cost_ref, rt_ref, cells_ref, costs_ref, wind_planes_ref)
        move_tracers(t_ref, ends_ref, middle_ref, gm_ref, r0_ref, r3_ref, None, t_out, planes_ref, edges)
        states = [entries(p, cells_ref, rt_ref, planes_ref) for p in range(2)]
        for p in range(2):
            x0_ref[p] = states[p]
        all_columns(states, costs_ref, wi_ref, wo_ref, turned_ref)


def correct(
    early, to_left_ref, to_right_ref, cl_ref, cr_ref, costs_ref, wi_ref, wo_ref, t_out, turned_ref, store
):
    te_ref, x0_ref, before_turned_ref, *edges = early
    lane = lane_index((128, 128))
    changes = []
    for side, (own_ref, other_ref) in enumerate(((to_left_ref, cl_ref), (to_right_ref, cr_ref))):
        total = own_ref[...].astype(f32) + pltpu.roll(other_ref[...].astype(f32), 124 if side else 4, 1)
        ours = lane_index((1, 128)) >= 124 if side else lane_index((1, 128)) < 4
        scale = jnp.where(ours, time_step / jnp.where(ours, total[128:129], 1.0), 0.0)
        new = edges[side][...] + total[:128] * scale
        delta = jnp.where(ours, new - edges[2 + side][...], 0.0).astype(bf16)
        weights = jnp.zeros((8, 128), f32)
        row = lax.broadcasted_iota(jnp.int32, (8, 128), 0)
        for p in range(2):
            for a in range(4):
                place = jnp.logical_and(row == p, lane_index((8, 128)) == (124 + a if side else a))
                weights = jnp.where(place, remap_table[p][a] * remap_table[0][0], weights)
        high = weights.astype(bf16)
        low = (weights - high.astype(f32)).astype(bf16)
        changes.append(
            lax.dot_general(high, delta, NT, preferred_element_type=f32)
            + lax.dot_general(low, delta, NT, preferred_element_type=f32)
        )
        for a in range(4):
            rows = pl.ds(side * 4 + row_of(a), 128, stride=8)
            moved = pltpu.roll(new, 3 - a if side else (128 - a) % 128, 1)
            t_out[rows, :] = jnp.where(lane == (127 if side else 0), moved, te_ref[rows, :])
    store.start()
    row = lax.broadcasted_iota(jnp.int32, (8, 256), 0)
    states, costs = [], []
    for p in range(2):
        ends = []
        for side in range(2):
            change = jnp.concatenate([changes[side][p : p + 1], jnp.zeros((1, 128), f32)], axis=1)
            ends.append(x0_ref[p, side * 120 : side * 120 + 8, :] + change)
        states.append(jnp.where(row == 0, ends[0], ends[1]))
        first = pl.multiple_of(cell_row(p) * 128, 128)
        ends = [jnp.concatenate([costs_ref[pl.ds(first + side * 120, 8), :]] * 2, axis=1) for side in range(2)]
        costs.append(jnp.where(row == 0, ends[0], ends[1]))
    (state,) = network(
        [jnp.concatenate(states, axis=0)], [jnp.concatenate(costs, axis=0)], wi_ref, wo_ref
    )
    for p in range(2):
        part = state[p * 8 : (p + 1) * 8]
        top, bottom = jnp.where(row == 0, part, 0.0), jnp.where(row == 7, part, 0.0)
        placed = turn(jnp.concatenate([top, jnp.zeros((112, 256), f32), bottom], axis=0))
        rows = pl.ds(cell_row(p), 256, stride=2)
        column = lane_index((256, 128))
        changed = jnp.logical_or(column == 0, column == 127)
        turned_ref[rows, :] = jnp.where(changed, placed, before_turned_ref[rows, :])


def finish_kernel(
    t_ref, ends_ref, middle_ref, gm_ref, r0_ref, r3_ref, cl_ref, cr_ref, to_left_ref, to_right_ref, cells_ref,
    costs_ref, rt_ref, wi_ref, wo_ref, *rest,
):
    *early, t_hbm, c_hbm, planes_ref, turned_ref, t_out, c_out, sems = rest
    store = pltpu.make_async_copy(t_out, t_hbm, sems.at[0])
    ahead = works_early()

    @pl.when(ahead)
    def _():
        correct(
            early, to_left_ref, to_right_ref, cl_ref, cr_ref, costs_ref, wi_ref, wo_ref, t_out, turned_ref, store
        )

    @pl.when(jnp.logical_not(ahead))
    def _():
        columns = (cl_ref, cr_ref)
        move_tracers(t_ref, ends_ref, middle_ref, gm_ref, r0_ref, r3_ref, columns, t_out, planes_ref)
        store.start()
        states = [entries(p, cells_ref, rt_ref, planes_ref) for p in range(2)]
        all_columns(states, costs_ref, wi_ref, wo_ref, turned_ref)

    c_out[...] = turned_ref[...].astype(bf16)
    final = pltpu.make_async_copy(c_out, c_hbm, sems.at[1])
    final.start()
    store.wait()
    final.wait()


def call(kernel, outs, scratch, name, hbm_in=(), hbm_out=(), semaphores=0):
    shapes = tuple(jax.ShapeDtypeStruct(*o) for o in outs)
    scratch = [pltpu.VMEM(*s) for s in scratch]
    if semaphores:
        scratch.append(pltpu.SemaphoreType.DMA((semaphores,)))

    def spec(in_hbm):
        return pl.BlockSpec(memory_space=pltpu.HBM if in_hbm else pltpu.VMEM)

    def run(*args):
        args = [
            pltpu.with_memory_space_constraint(x, pltpu.HBM) if i in hbm_in else x
            for i, x in enumerate(args)
        ]
        return pl.pallas_call(
            kernel,
            out_shape=shapes,
            in_specs=[spec(i in hbm_in) for i in range(len(args))],
            out_specs=tuple(spec(i in hbm_out) for i in range(len(outs))),
            scratch_shapes=scratch,
            compiler_params=pltpu.CompilerParams(vmem_limit_bytes=24 * 1024 * 1024),
            name=name,
        )(*args)

    return run


def node_rows(array):
    k, levels = array.shape[:2]
    return array.reshape(k, levels, 4, 2, 128).transpose(0, 1, 3, 2, 4).reshape(k * levels * 8, 128)


def shift(value, axis, by):
    count = lax.axis_size(axis)
    return lax.ppermute(value, axis, [(i, (i + by) % count) for i in range(count)])


def shards(tracers, winds, node_mass, column_cost, weight_in, weight_out):
    t = node_rows(tracers)
    w = node_rows(winds)
    m = node_mass.reshape(4, 2, 128).transpose(1, 0, 2).reshape(8, 128)
    column, message = ((ROWS, 128), f32), ((ROWS, 256), bf16)
    pair, nodes = ((2, 128, 256), f32), ((1024, 128), f32)
    t, wf, mass, dy, ends, gm, outer, inner = call(
        tendency_kernel,
        [nodes, nodes, ((8, 128), f32), ((256, 256), bf16), pair, ((4, 256), f32), message, message],
        [((1024, 128), bf16), ((8, 128), f32)],
        "tendency",
        hbm_in=(0, 1, 2, 3),
        semaphores=4,
    )(t, w, m, jnp.asarray(lane_derivative()))
    middle, left, right = call(middle_kernel, [pair, column, column], [], "middle")(
        t, wf, mass, dy, gm, ends
    )
    count = lax.axis_size("grp")
    r0 = lax.ppermute(outer, "grp", [(i, (i + (1 if i % 2 else -1)) % count) for i in range(count)])
    r3 = lax.ppermute(inner, "grp", [(i, i ^ 1) for i in range(count)])
    column = ((ROWS, 128), bf16)
    to_left, to_right = call(edges_kernel, [column, column], [], "edges")(left, right, r0, r3)
    remap = jnp.asarray(lane_remap())
    cells, costs, small = ((256, 128), bf16), ((256, 128), f32), ((128, 128), f32)
    weights = [((256, 1024), bf16), ((1024, 256), bf16)]
    early = call(
        early_kernel,
        [nodes, ((2, 128, 256), f32), ((512, 128), f32), small, small, small, small],
        [((2, 128, 256), bf16), ((2, 128, 256), bf16), cells, costs, ((2, 128), jnp.int32), ((256, 256), bf16), *weights],
        "early",
        hbm_in=(7, 8, 9, 10),
        semaphores=4,
    )(t, ends, middle, gm, r0, r3, wf, column_cost, remap, weight_in, weight_out)
    to_left, to_right, *early = lax.optimization_barrier((to_left, to_right, *early))
    cl = shift(to_right, "bal", 1)
    cr = shift(to_left, "bal", -1)
    cells, costs, first_weights, second_weights = call(
        beside_kernel,
        [cells, costs, *weights],
        [((2, 128, 256), bf16)],
        "winds",
        hbm_in=(3, 4),
        semaphores=2,
    )(wf, column_cost, remap, weight_in, weight_out, to_left)
    t_next, columns = call(
        finish_kernel,
        [((1024, 128), f32), ((512, 128), bf16)],
        [((2, 128, 256), bf16), ((512, 128), f32), ((1024, 128), f32), ((512, 128), bf16)],
        "finish",
        hbm_out=(0, 1),
        semaphores=2,
    )(
        t, ends, middle, gm, r0, r3, cl, cr, to_left, to_right, cells, costs, remap, first_weights,
        second_weights, *early,
    )
    t_next = t_next.reshape(2, 64, 2, 4, 128).transpose(0, 1, 3, 2, 4).reshape(2, 64, 4, 256)
    return t_next, columns.reshape(4, 64, 2, 128)


def solution(mesh):
    placed = (
        P(None, None, "grp", "bal"),
        P(None, None, "grp", "bal"),
        P("grp", "bal"),
        P("grp", "bal"),
        P(),
        P(),
    )
    return jax.shard_map(
        shards,
        mesh=mesh,
        in_specs=placed,
        out_specs=(P(None, None, "grp", "bal"), P(None, None, "grp", "bal")),
        check_vma=False,
    )
```

```python
import functools

import jax
import jax.numpy as jnp
import ml_dtypes
import numpy as np
from jax import lax
from jax.experimental import pallas as pl
from jax.experimental.pallas import tpu as pltpu
from jax.sharding import PartitionSpec as P

time_step = 0.02
remap_table = ((0.45, 0.4, 0.15, 0.0), (0.0, 0.15, 0.4, 0.45))
gll_points = (-1.0, -0.4472135954999579, 0.4472135954999579, 1.0)
f32, bf16 = jnp.float32, jnp.bfloat16
CHUNK = 16
ROWS = 144
NT = (((1,), (1,)), ((), ()))


def gll_matrix():
    matrix = []
    for row_idx in range(4):
        entries = []
        for col_idx in range(4):
            if row_idx == col_idx:
                running = 0.0
                for third_idx in range(4):
                    if third_idx != row_idx:
                        running += 1.0 / (gll_points[row_idx] - gll_points[third_idx])
                entries.append(2.0 * running)
            else:
                numerator = 1.0
                denominator = 1.0
                for third_idx in range(4):
                    if third_idx != row_idx:
                        numerator *= gll_points[row_idx] - gll_points[third_idx]
                    if third_idx != col_idx:
                        denominator *= gll_points[col_idx] - gll_points[third_idx]
                entries.append(
                    2.0 * numerator / (denominator * (gll_points[row_idx] - gll_points[col_idx]))
                )
        matrix.append(entries)
    return matrix


def split_bf16(values):
    high = values.astype(np.float32).astype(ml_dtypes.bfloat16)
    low = (values.astype(np.float32) - high.astype(np.float32)).astype(ml_dtypes.bfloat16)
    return high, low


def lane_derivative():
    block = np.kron(np.eye(32), np.array(gll_matrix()).T)
    high, low = split_bf16(block)
    return np.block([[high, low], [high, np.zeros_like(low)]])


def lane_remap():
    high, low = split_bf16(np.kron(np.eye(64), np.array(remap_table)))
    return np.concatenate([high, low], axis=0)


def lane_index(shape):
    return lax.broadcasted_iota(jnp.int32, shape, 1)


def assemble_lanes(values):
    lane = lane_index(values.shape)
    inside = lane % 4
    first = jnp.logical_and(inside == 0, lane > 0)
    last = jnp.logical_and(inside == 3, lane < values.shape[1] - 1)
    return (
        values
        + jnp.where(first, pltpu.roll(values, 1, 1), 0.0)
        + jnp.where(last, pltpu.roll(values, values.shape[1] - 1, 1), 0.0)
    )


def edge_columns(planes):
    lane = lane_index((planes[0].shape[0], 128))
    left = jnp.zeros(lane.shape, f32)
    right = jnp.zeros(lane.shape, f32)
    for a in range(4):
        low, high = planes[a][:, :128], planes[a][:, 128:]
        left = jnp.where(lane == a, pltpu.roll(low, a, 1) if a else low, left)
        right = jnp.where(lane == 124 + a, pltpu.roll(high, 125 + a, 1) if a < 3 else high, right)
    return left, right


def row_of(a):
    odd = lax.axis_index("grp") % 2
    return a + odd * (3 - 2 * a)


def weighted_rows(rows, channel, t_ref, wf_ref, mass, dy_ref):
    derivative = gll_matrix()
    sign = jnp.where(lax.axis_index("grp") % 2 == 1, -1.0, 1.0)
    level = channel % 64
    x = {
        (a, j): t_ref[pl.ds(channel * 8 + j * 4 + row_of(a), CHUNK, stride=8), :]
        for a in range(4)
        for j in range(2)
    }
    lhs = []
    for a in rows:
        for j in range(2):
            high = x[a, j].astype(bf16)
            low = (x[a, j] - high.astype(f32)).astype(bf16)
            lhs.append(jnp.concatenate([high, low], axis=1))
    product = jnp.dot(jnp.concatenate(lhs, axis=0), dy_ref[...], preferred_element_type=f32)
    along_y = product[:, :128] + product[:, 128:]
    planes = []
    for n, a in enumerate(rows):
        halves = []
        for j in range(2):
            along_x = derivative[a][0] * x[0, j]
            for b in range(1, 4):
                along_x += derivative[a][b] * x[b, j]
            position = (2 * n + j) * CHUNK
            u = wf_ref[pl.ds(level * 8 + j * 4 + row_of(a), CHUNK, stride=8), :]
            v = wf_ref[pl.ds(512 + level * 8 + j * 4 + row_of(a), CHUNK, stride=8), :]
            total = (sign * u) * along_x + v * along_y[position : position + CHUNK]
            halves.append(-total * mass[j * 4 + a : j * 4 + a + 1, :])
        planes.append(assemble_lanes(jnp.concatenate(halves, axis=1)))
    return planes


def tendency_kernel(
    t_hbm, w_hbm, m_hbm, dy_hbm, t_ref, wf_ref, mass_ref, dy_ref, g_ref, gm_ref, outer_ref, inner_ref,
    w_ref, m_ref, sems,
):
    copies = [
        pltpu.make_async_copy(source, target, sems.at[i])
        for i, (source, target) in enumerate(
            [(w_hbm, w_ref), (t_hbm, t_ref), (m_hbm, m_ref), (dy_hbm, dy_ref)]
        )
    ]
    for copy in copies:
        copy.start()
    copies[2].wait()
    mass = m_ref[...]
    backward = jnp.concatenate([mass[i : i + 1] for i in (3, 2, 1, 0, 7, 6, 5, 4)], axis=0)
    mass = jnp.where(lax.axis_index("grp") % 2 == 1, backward, mass)
    mass_ref[...] = mass
    mass_rows = assemble_lanes(jnp.concatenate([mass[0:4], mass[4:8]], axis=1))
    gm_ref[...] = mass_rows
    pad = jnp.zeros((ROWS - 129, 256), f32)
    outer_ref[128:, :] = jnp.concatenate([mass_rows[0:1], pad], axis=0).astype(bf16)
    inner_ref[128:, :] = jnp.concatenate([mass_rows[3:4], pad], axis=0).astype(bf16)
    copies[0].wait()
    wf_ref[...] = w_ref[...].astype(f32)
    copies[1].wait()
    copies[3].wait()
    for channel in range(0, 128, CHUNK):
        rows = slice(channel, channel + CHUNK)
        planes = weighted_rows((0, 3), channel, t_ref, wf_ref, mass, dy_ref)
        for n, target in enumerate((outer_ref, inner_ref)):
            g_ref[n, rows, :] = planes[n]
            target[rows, :] = planes[n].astype(bf16)


def middle_kernel(t_ref, wf_ref, mass_ref, dy_ref, gm_ref, ends_ref, g_ref, left_ref, right_ref):
    mass = mass_ref[...]
    row_left, row_right = edge_columns([gm_ref[a : a + 1, :] for a in range(4)])
    pad = jnp.zeros((ROWS - 129, 128), f32)
    left_ref[128:, :] = jnp.concatenate([row_left, pad], axis=0)
    right_ref[128:, :] = jnp.concatenate([row_right, pad], axis=0)
    for channel in range(0, 128, CHUNK):
        rows = slice(channel, channel + CHUNK)
        planes = weighted_rows((1, 2), channel, t_ref, wf_ref, mass, dy_ref)
        for n in range(2):
            g_ref[n, rows, :] = planes[n]
        left, right = edge_columns([ends_ref[0, rows, :], *planes, ends_ref[1, rows, :]])
        left_ref[rows, :] = left
        right_ref[rows, :] = right


def wind_cells(wf_ref, cost_ref, rt_ref, cells_ref, costs_ref, planes_ref):
    for k in range(2):
        for group in range(64 // CHUNK):
            channel = k * 64 + group * CHUNK
            sums = [None, None]
            for a in range(4):
                row = jnp.concatenate(
                    [wf_ref[pl.ds(channel * 8 + j * 4 + a, CHUNK, stride=8), :] for j in range(2)],
                    axis=1,
                )
                for p in range(2):
                    if remap_table[p][a]:
                        term = remap_table[p][a] * row
                        sums[p] = term if sums[p] is None else sums[p] + term
            for p in range(2):
                planes_ref[p, channel : channel + CHUNK, :] = sums[p].astype(bf16)
    eye = lax.broadcasted_iota(jnp.int32, (128, 128), 0) == lane_index((128, 128))
    for p in range(2):
        product = lax.dot_general(rt_ref[...], planes_ref[p], NT, preferred_element_type=f32)
        cells_ref[p * 128 : (p + 1) * 128, :] = (product[:128] + product[128:]).astype(bf16)
        diagonal = jnp.where(eye, cost_ref[p : p + 1, :].astype(f32), 0.0).astype(bf16)
        costs_ref[p * 128 : (p + 1) * 128, :] = jnp.dot(
            diagonal, jnp.ones((128, 128), bf16), preferred_element_type=f32
        )


def beside_kernel(
    wf_ref, cost_ref, rt_ref, wi_hbm, wo_hbm, after_ref, cells_ref, costs_ref, wi_ref, wo_ref, planes_ref, sems
):
    first = pltpu.make_async_copy(wi_hbm, wi_ref, sems.at[0])
    second = pltpu.make_async_copy(wo_hbm, wo_ref, sems.at[1])
    first.start()
    second.start()
    wind_cells(wf_ref, cost_ref, rt_ref, cells_ref, costs_ref, planes_ref)
    first.wait()
    second.wait()


def with_columns(a, own, cl, cr):
    lane = lane_index(cl.shape)
    left = jnp.where(lane == 0, pltpu.roll(cl, 4 - a, 1), 0.0)
    right = jnp.where(lane == 127, pltpu.roll(cr, 127 - a, 1), 0.0)
    return jnp.concatenate([own[:, :128] + left, own[:, 128:] + right], axis=1)


def edges_kernel(left_ref, right_ref, r0_ref, r3_ref, to_left_ref, to_right_ref):
    lane = lane_index((ROWS, 128))
    r0 = r0_ref[...].astype(f32)
    r3 = r3_ref[...].astype(f32)
    left = left_ref[...] + jnp.where(lane == 0, r0[:, :128], 0.0)
    left += jnp.where(lane == 3, pltpu.roll(r3[:, :128], 3, 1), 0.0)
    right = right_ref[...] + jnp.where(lane == 127, r3[:, 128:], 0.0)
    right += jnp.where(lane == 124, pltpu.roll(r0[:, 128:], 125, 1), 0.0)
    to_left_ref[...] = left.astype(bf16)
    to_right_ref[...] = right.astype(bf16)


def gelu(x):
    inner = x * (0.7978845608028654 + 0.035677408136300125 * (x * x))
    half = 0.5 * x
    return half + half * jnp.tanh(inner)


def cell_row(p):
    odd = lax.axis_index("grp") % 2
    return p + odd * (1 - 2 * p)


def works_early():
    me, last = lax.axis_index("grp"), lax.axis_size("grp") - 1
    return jnp.logical_and(lax.axis_index("bal") == 0, jnp.logical_and(me > 0, me < last - 1))


def move_tracers(t_ref, ends_ref, middle_ref, gm_ref, r0_ref, r3_ref, columns, t_out, planes_ref, edges=None):
    def complete(a, own, start, size):
        rows = slice(start, start + CHUNK)
        if a in (0, 3):
            own += (r0_ref if a == 0 else r3_ref)[rows, :].astype(f32)[:size]
        if columns is None:
            return own
        return with_columns(a, own, *(ref[rows, :].astype(f32)[:size] for ref in columns))

    scale = [time_step / complete(a, gm_ref[a : a + 1, :], 128, 1) for a in range(4)]
    for channel in range(0, 128, CHUNK):
        here = slice(channel, channel + CHUNK)
        sums = [None, None]
        before, after = [], []
        for a in range(4):
            source, n = (ends_ref, a // 3) if a in (0, 3) else (middle_ref, a - 1)
            change = complete(a, source[n, here, :], channel, CHUNK) * scale[a]
            old, new = [], []
            for j in range(2):
                rows = pl.ds(channel * 8 + j * 4 + row_of(a), CHUNK, stride=8)
                old.append(t_ref[rows, :])
                new.append(old[j] + change[:, j * 128 : (j + 1) * 128])
                t_out[rows, :] = new[j]
            row = jnp.concatenate(new, axis=1)
            before.append(jnp.concatenate(old, axis=1))
            after.append(row)
            for p in range(2):
                if remap_table[p][a]:
                    term = remap_table[p][a] * row
                    sums[p] = term if sums[p] is None else sums[p] + term
        for p in range(2):
            planes_ref[p, here, :] = sums[p].astype(bf16)
        if edges is not None:
            for target, values in zip(edges, (*edge_columns(before), *edge_columns(after))):
                target[here, :] = values


def own_cells(p):
    return pl.ds(pl.multiple_of(cell_row(p) * 128, 128), 128)


def entries(p, cells_ref, rt_ref, planes_ref):
    product = lax.dot_general(rt_ref[...], planes_ref[p], NT, preferred_element_type=f32)
    return jnp.concatenate([product[:128] + product[128:], cells_ref[own_cells(p), :].astype(f32)], axis=1)


def network(states, costs, wi_ref, wo_ref):
    states = [state.astype(bf16).astype(f32) for state in states]
    for substep in range(3):
        for p in range(len(states)):
            rounded = states[p].astype(bf16)
            stepped = states[p]
            for h in range(0, 1024, 256):
                hidden = jnp.dot(rounded, wi_ref[:, h : h + 256], preferred_element_type=f32)
                stepped += jnp.dot(
                    gelu(hidden).astype(bf16), wo_ref[h : h + 256, :], preferred_element_type=f32
                )
            states[p] = jnp.where(costs[p] > substep, stepped, states[p])
    return states


def turn(values):
    eye = lax.broadcasted_iota(jnp.int32, (256, 256), 0) == lane_index((256, 256))
    return lax.dot_general(
        jnp.where(eye, 1.0, 0.0).astype(bf16), values.astype(bf16), NT, preferred_element_type=f32
    )


def all_columns(states, costs_ref, wi_ref, wo_ref, turned_ref):
    costs = [jnp.concatenate([costs_ref[own_cells(p), :]] * 2, axis=1) for p in range(2)]
    for p, state in enumerate(network(states, costs, wi_ref, wo_ref)):
        turned_ref[pl.ds(cell_row(p), 256, stride=2), :] = turn(state)


def early_kernel(
    t_ref, ends_ref, middle_ref, gm_ref, r0_ref, r3_ref, wf_ref, cost_hbm, rt_hbm, wi_hbm, wo_hbm,
    t_out, x0_ref, turned_ref, *rest,
):
    *edges, planes_ref, wind_planes_ref, cells_ref, costs_ref, cost_ref, rt_ref, wi_ref, wo_ref, sems = rest

    @pl.when(works_early())
    def _():
        sources, targets = (cost_hbm, rt_hbm, wi_hbm, wo_hbm), (cost_ref, rt_ref, wi_ref, wo_ref)
        copies = [pltpu.make_async_copy(*pair, sems.at[i]) for i, pair in enumerate(zip(sources, targets))]
        for copy in copies:
            copy.start()
        for copy in copies:
            copy.wait()
        wind_cells(wf_ref, cost_ref, rt_ref, cells_ref, costs_ref, wind_planes_ref)
        move_tracers(t_ref, ends_ref, middle_ref, gm_ref, r0_ref, r3_ref, None, t_out, planes_ref, edges)
        states = [entries(p, cells_ref, rt_ref, planes_ref) for p in range(2)]
        for p in range(2):
            x0_ref[p] = states[p]
        all_columns(states, costs_ref, wi_ref, wo_ref, turned_ref)


def correct(
    early, to_left_ref, to_right_ref, cl_ref, cr_ref, costs_ref, wi_ref, wo_ref, t_out, turned_ref, store
):
    te_ref, x0_ref, before_turned_ref, *edges = early
    lane = lane_index((128, 128))
    changes = []
    for side, (own_ref, other_ref) in enumerate(((to_left_ref, cl_ref), (to_right_ref, cr_ref))):
        total = own_ref[...].astype(f32) + pltpu.roll(other_ref[...].astype(f32), 124 if side else 4, 1)
        ours = lane_index((1, 128)) >= 124 if side else lane_index((1, 128)) < 4
        scale = jnp.where(ours, time_step / jnp.where(ours, total[128:129], 1.0), 0.0)
        new = edges[side][...] + total[:128] * scale
        delta = jnp.where(ours, new - edges[2 + side][...], 0.0).astype(bf16)
        weights = jnp.zeros((8, 128), f32)
        row = lax.broadcasted_iota(jnp.int32, (8, 128), 0)
        for p in range(2):
            for a in range(4):
                place = jnp.logical_and(row == p, lane_index((8, 128)) == (124 + a if side else a))
                weights = jnp.where(place, remap_table[p][a] * remap_table[0][0], weights)
        high = weights.astype(bf16)
        low = (weights - high.astype(f32)).astype(bf16)
        changes.append(
            lax.dot_general(high, delta, NT, preferred_element_type=f32)
            + lax.dot_general(low, delta, NT, preferred_element_type=f32)
        )
        for a in range(4):
            rows = pl.ds(side * 4 + row_of(a), 128, stride=8)
            moved = pltpu.roll(new, 3 - a if side else (128 - a) % 128, 1)
            t_out[rows, :] = jnp.where(lane == (127 if side else 0), moved, te_ref[rows, :])
    store.start()
    row = lax.broadcasted_iota(jnp.int32, (8, 256), 0)
    states, costs = [], []
    for p in range(2):
        ends = []
        for side in range(2):
            change = jnp.concatenate([changes[side][p : p + 1], jnp.zeros((1, 128), f32)], axis=1)
            ends.append(x0_ref[p, side * 120 : side * 120 + 8, :] + change)
        states.append(jnp.where(row == 0, ends[0], ends[1]))
        first = pl.multiple_of(cell_row(p) * 128, 128)
        ends = [jnp.concatenate([costs_ref[pl.ds(first + side * 120, 8), :]] * 2, axis=1) for side in range(2)]
        costs.append(jnp.where(row == 0, ends[0], ends[1]))
    (state,) = network(
        [jnp.concatenate(states, axis=0)], [jnp.concatenate(costs, axis=0)], wi_ref, wo_ref
    )
    for p in range(2):
        part = state[p * 8 : (p + 1) * 8]
        top, bottom = jnp.where(row == 0, part, 0.0), jnp.where(row == 7, part, 0.0)
        placed = turn(jnp.concatenate([top, jnp.zeros((112, 256), f32), bottom], axis=0))
        rows = pl.ds(cell_row(p), 256, stride=2)
        column = lane_index((256, 128))
        changed = jnp.logical_or(column == 0, column == 127)
        turned_ref[rows, :] = jnp.where(changed, placed, before_turned_ref[rows, :])


def finish_kernel(
    t_ref, ends_ref, middle_ref, gm_ref, r0_ref, r3_ref, cl_ref, cr_ref, to_left_ref, to_right_ref, cells_ref,
    costs_ref, rt_ref, wi_ref, wo_ref, *rest,
):
    *early, t_hbm, c_hbm, planes_ref, turned_ref, t_out, c_out, sems = rest
    store = pltpu.make_async_copy(t_out, t_hbm, sems.at[0])
    ahead = works_early()

    @pl.when(ahead)
    def _():
        correct(
            early, to_left_ref, to_right_ref, cl_ref, cr_ref, costs_ref, wi_ref, wo_ref, t_out, turned_ref, store
        )

    @pl.when(jnp.logical_not(ahead))
    def _():
        columns = (cl_ref, cr_ref)
        move_tracers(t_ref, ends_ref, middle_ref, gm_ref, r0_ref, r3_ref, columns, t_out, planes_ref)
        store.start()
        states = [entries(p, cells_ref, rt_ref, planes_ref) for p in range(2)]
        all_columns(states, costs_ref, wi_ref, wo_ref, turned_ref)

    c_out[...] = turned_ref[...].astype(bf16)
    final = pltpu.make_async_copy(c_out, c_hbm, sems.at[1])
    final.start()
    store.wait()
    final.wait()


def call(kernel, outs, scratch, name, hbm_in=(), hbm_out=(), semaphores=0):
    shapes = tuple(jax.ShapeDtypeStruct(*o) for o in outs)
    scratch = [pltpu.VMEM(*s) for s in scratch]
    if semaphores:
        scratch.append(pltpu.SemaphoreType.DMA((semaphores,)))

    def spec(in_hbm):
        return pl.BlockSpec(memory_space=pltpu.HBM if in_hbm else pltpu.VMEM)

    def run(*args):
        args = [
            pltpu.with_memory_space_constraint(x, pltpu.HBM) if i in hbm_in else x
            for i, x in enumerate(args)
        ]
        return pl.pallas_call(
            kernel,
            out_shape=shapes,
            in_specs=[spec(i in hbm_in) for i in range(len(args))],
            out_specs=tuple(spec(i in hbm_out) for i in range(len(outs))),
            scratch_shapes=scratch,
            compiler_params=pltpu.CompilerParams(vmem_limit_bytes=24 * 1024 * 1024),
            name=name,
        )(*args)

    return run


def node_rows(array):
    k, levels = array.shape[:2]
    return array.reshape(k, levels, 4, 2, 128).transpose(0, 1, 3, 2, 4).reshape(k * levels * 8, 128)


def shift(value, axis, by):
    count = lax.axis_size(axis)
    return lax.ppermute(value, axis, [(i, (i + by) % count) for i in range(count)])


def shards(tracers, winds, node_mass, column_cost, weight_in, weight_out):
    t = node_rows(tracers)
    w = node_rows(winds)
    m = node_mass.reshape(4, 2, 128).transpose(1, 0, 2).reshape(8, 128)
    column, message = ((ROWS, 128), f32), ((ROWS, 256), bf16)
    pair, nodes = ((2, 128, 256), f32), ((1024, 128), f32)
    t, wf, mass, dy, ends, gm, outer, inner = call(
        tendency_kernel,
        [nodes, nodes, ((8, 128), f32), ((256, 256), bf16), pair, ((4, 256), f32), message, message],
        [((1024, 128), bf16), ((8, 128), f32)],
        "tendency",
        hbm_in=(0, 1, 2, 3),
        semaphores=4,
    )(t, w, m, jnp.asarray(lane_derivative()))
    middle, left, right = call(middle_kernel, [pair, column, column], [], "middle")(
        t, wf, mass, dy, gm, ends
    )
    count = lax.axis_size("grp")
    r0 = lax.ppermute(outer, "grp", [(i, (i + (1 if i % 2 else -1)) % count) for i in range(count)])
    r3 = lax.ppermute(inner, "grp", [(i, i ^ 1) for i in range(count)])
    column = ((ROWS, 128), bf16)
    to_left, to_right = call(edges_kernel, [column, column], [], "edges")(left, right, r0, r3)
    remap = jnp.asarray(lane_remap())
    cells, costs, small = ((256, 128), bf16), ((256, 128), f32), ((128, 128), f32)
    weights = [((256, 1024), bf16), ((1024, 256), bf16)]
    early = call(
        early_kernel,
        [nodes, ((2, 128, 256), f32), ((512, 128), f32), small, small, small, small],
        [((2, 128, 256), bf16), ((2, 128, 256), bf16), cells, costs, ((2, 128), jnp.int32), ((256, 256), bf16), *weights],
        "early",
        hbm_in=(7, 8, 9, 10),
        semaphores=4,
    )(t, ends, middle, gm, r0, r3, wf, column_cost, remap, weight_in, weight_out)
    to_left, to_right, *early = lax.optimization_barrier((to_left, to_right, *early))
    cl = shift(to_right, "bal", 1)
    cr = shift(to_left, "bal", -1)
    cells, costs, first_weights, second_weights = call(
        beside_kernel,
        [cells, costs, *weights],
        [((2, 128, 256), bf16)],
        "winds",
        hbm_in=(3, 4),
        semaphores=2,
    )(wf, column_cost, remap, weight_in, weight_out, to_left)
    t_next, columns = call(
        finish_kernel,
        [((1024, 128), f32), ((512, 128), bf16)],
        [((2, 128, 256), bf16), ((512, 128), f32), ((1024, 128), f32), ((512, 128), bf16)],
        "finish",
        hbm_out=(0, 1),
        semaphores=2,
    )(
        t, ends, middle, gm, r0, r3, cl, cr, to_left, to_right, cells, costs, remap, first_weights,
        second_weights, *early,
    )
    t_next = t_next.reshape(2, 64, 2, 4, 128).transpose(0, 1, 3, 2, 4).reshape(2, 64, 4, 256)
    return t_next, columns.reshape(4, 64, 2, 128)


def solution(mesh):
    placed = (
        P(None, None, "grp", "bal"),
        P(None, None, "grp", "bal"),
        P("grp", "bal"),
        P("grp", "bal"),
        P(),
        P(),
    )
    return jax.shard_map(
        shards,
        mesh=mesh,
        in_specs=placed,
        out_specs=(P(None, None, "grp", "bal"), P(None, None, "grp", "bal")),
        check_vma=False,
    )
```
